768 devices in a mesh: blk: 384 (over x, z, y), grp: 2 (over core).
Axes of the slice: x: 4, y: 8, z: 12, core: 2. Of those that a mesh axis runs over, the one named last changes fastest.
Arguments:
- picture_embeddings: bfloat16 [98304, 1152], P('blk', 'grp')
- description_embeddings: bfloat16 [98304, 1152], P('blk', 'grp')
- sharpness_factor: float32 [1], replicated, may hold values from 10 to 30
- offset_term: float32 [1], replicated, may hold values from -3 to -1
Outputs:
- grad_image: float32 [98304, 1152], P('blk', 'grp')
- grad_text: float32 [98304, 1152], P('blk', 'grp')
The draws below stay inside these ranges and needn't reach their ends.
All inputs are finite; a program needn't handle non-finite values.
Results may differ from the reference program's by a relative error of at most 0.0024.
Values may be sent and summed in bfloat16 or wider, within the bound.
A program may use at most 32 MiB of HBM per device.

```python
import math
import jax
import jax.numpy as jnp

D = 1152
ROWS = 256
HOPS = 8
PAIRS = 98304
N_BLK = 384


def shared_portion(key):
    base = jax.random.normal(key, (PAIRS, D), jnp.float32)
    return jnp.clip(base, -6.0, 6.0)


def draw_picture_embeddings(key, part):
    common = shared_portion(key)
    key = jax.random.fold_in(key, 11)
    own = jnp.clip(jax.random.normal(key, (PAIRS, D), jnp.float32), -6.0, 6.0)
    return ((0.8 * common + 0.6 * own) / jnp.sqrt(float(D))).astype(jnp.bfloat16)


def draw_description_embeddings(key, part):
    common = shared_portion(key)
    key = jax.random.fold_in(key, 23)
    own = jnp.clip(jax.random.normal(key, (PAIRS, D), jnp.float32), -6.0, 6.0)
    return ((0.8 * common + 0.6 * own) / jnp.sqrt(float(D))).astype(jnp.bfloat16)


def setup_inputs(seed: int = 0) -> dict:
    key_list = jax.random.split(jax.random.key(seed), 5)
    return {
        "picture_embeddings": draw_picture_embeddings(jax.random.fold_in(key_list[4], 71), 0),
        "description_embeddings": draw_description_embeddings(jax.random.fold_in(key_list[4], 71), 0),
        "sharpness_factor": jnp.clip(jnp.exp(jax.random.uniform(key_list[2], (1,), jnp.float32, math.log(10.0), math.log(30.0))), 10.0, 30.0),
        "offset_term": jnp.clip(jax.random.uniform(key_list[3], (1,), jnp.float32, -3.0, -1.0), -3.0, -1.0),
    }


def reference(picture_embeddings, description_embeddings, sharpness_factor, offset_term):
    similarity_multiplier = sharpness_factor[0]
    offset = offset_term[0]
    width = picture_embeddings.shape[1]
    images = picture_embeddings.reshape(N_BLK, ROWS, width)
    texts = description_embeddings.reshape(N_BLK, ROWS, width)
    image_rows_float = images.astype(jnp.float32)
    identity_matches = (jnp.arange(ROWS, dtype=jnp.int32)[:, None] == jnp.arange(ROWS, dtype=jnp.int32)[None, :]).astype(jnp.float32)
    grad_image = jnp.zeros((N_BLK, ROWS, width), jnp.float32)
    grad_text = jnp.zeros((N_BLK, ROWS, width), jnp.float32)
    for hop in range(HOPS):
        rolled = jnp.roll(texts, hop, axis=0)
        rolled_f = rolled.astype(jnp.float32)
        dots = jnp.einsum("brd,bcd->brc", image_rows_float, rolled_f)
        target_labels = identity_matches if hop == 0 else jnp.zeros_like(identity_matches)
        pair_coefficient = (similarity_multiplier * (jax.nn.sigmoid(similarity_multiplier * dots + offset) - target_labels[None])).astype(jnp.bfloat16)
        weight_f = pair_coefficient.astype(jnp.float32)
        grad_image = grad_image + jnp.einsum("brc,bcd->brd", weight_f, rolled_f)
        terms = jnp.einsum("brc,brd->bcd", weight_f, image_rows_float)
        grad_text = grad_text + jnp.roll(terms, -hop, axis=0)
    return grad_image.reshape(picture_embeddings.shape[0], width), grad_text.reshape(description_embeddings.shape[0], width)
```

```python
import functools

import jax
import jax.numpy as jnp
from jax import lax
from jax.experimental import pallas as pl
from jax.experimental.pallas import tpu as pltpu
from jax.sharding import PartitionSpec as P

HOPS = 8
PIECES = 4
SLOTS = 2 * HOPS
MESH = pl.DeviceIdType.MESH


def kernel(
    n,
    scale_ref,
    offset_ref,
    image_ref,
    text_ref,
    out_ref,
    blocks,
    own,
    sent,
    got,
    first_sem,
    send_sem,
    recv_sem,
    core_send_sem,
    core_recv_sem,
):
    me = lax.axis_index("blk")
    core = lax.axis_index("grp")
    width, rows = image_ref.shape
    piece = width // PIECES
    ahead, behind = lax.rem(me + 1, n), lax.rem(me + n - 1, n)
    far_ahead, far_behind = lax.rem(me + 7, n), lax.rem(me + n - 7, n)
    partner = (me, 1 - core)

    barrier = pltpu.get_barrier_semaphore()
    others = [(ahead, core), (behind, core), (far_ahead, core), (far_behind, core), partner]
    for other in others:
        pl.semaphore_signal(barrier, inc=1, device_id=other, device_id_type=MESH)
    pl.semaphore_wait(barrier, len(others))

    def part(j):
        return pl.ds(pl.multiple_of(j * piece, 16), piece)

    def first_copy(k, j):
        to = (ahead, behind, far_ahead, far_behind)[k]
        source = image_ref if k % 2 else text_ref
        return pltpu.make_async_remote_copy(
            src_ref=source.at[part(j)],
            dst_ref=blocks.at[2 + k, part(j)],
            send_sem=first_sem.at[k, j],
            recv_sem=recv_sem.at[2 + k, j],
            device_id=(to, core),
            device_id_type=MESH,
        )

    def next_copy(k, s, j):
        to = ahead if k in (0, 3) else behind
        t = 2 + 4 * s + k
        return pltpu.make_async_remote_copy(
            src_ref=blocks.at[t, part(j)],
            dst_ref=blocks.at[t + 4, part(j)],
            send_sem=send_sem.at[t, j],
            recv_sem=recv_sem.at[t + 4, j],
            device_id=(to, core),
            device_id_type=MESH,
        )

    def core_copy(t):
        return pltpu.make_async_remote_copy(
            src_ref=sent.at[t],
            dst_ref=got.at[t],
            send_sem=core_send_sem.at[t],
            recv_sem=core_recv_sem.at[t],
            device_id=partner,
            device_id_type=MESH,
        )

    for j in range(PIECES):
        for k in range(4):
            first_copy(k, j).start()

    blocks[0] = text_ref[...]
    blocks[1] = image_ref[...]
    own[0] = image_ref[...].T
    own[1] = text_ref[...].T
    scale, offset = scale_ref[0], offset_ref[0]

    def dots(t):
        sent[t] = jnp.dot(own[lax.rem(t, 2)], blocks[t], preferred_element_type=jnp.float32)
        core_copy(t).start()

    def grads(t, match):
        core_copy(t).wait()
        probs = jax.nn.sigmoid(scale * (sent[t] + got[t]) + offset)
        if match:
            row = lax.broadcasted_iota(jnp.int32, (rows, rows), 0)
            column = lax.broadcasted_iota(jnp.int32, (rows, rows), 1)
            probs = probs - (row == column).astype(jnp.float32)
        weight = (scale * probs).astype(jnp.bfloat16)
        term = lax.dot_general(
            blocks[t], weight, (((1,), (1,)), ((), ())), preferred_element_type=jnp.float32
        )
        side = lax.rem(t, 2)
        if match:
            out_ref[side] = term
        else:
            out_ref[side] = out_ref[side] + term

    dots(0)
    dots(1)
    grads(0, True)
    grads(1, True)

    @pl.loop(0, 4 * PIECES)
    def _(i):
        s, j = i // PIECES, lax.rem(i, PIECES)
        for k in range(4):

            @pl.when(s < (4 if k < 2 else 3))
            def _():
                t = 2 + 4 * s + k
                pltpu.make_async_remote_copy(
                    src_ref=blocks.at[t, part(j)],
                    dst_ref=blocks.at[t, part(j)],
                    send_sem=send_sem.at[t, j],
                    recv_sem=recv_sem.at[t, j],
                    device_id=(behind, core),
                    device_id_type=MESH,
                ).wait_recv()

            @pl.when(s < (3 if k < 2 else 2))
            def _():
                next_copy(k, s, j).start()

        @pl.when(s > 0)
        def _():
            t = i - PIECES + 2
            dots(t)

            @pl.when(t > 2)
            def _():
                grads(t - 1, False)

    dots(SLOTS - 2)
    grads(SLOTS - 3, False)
    dots(SLOTS - 1)
    grads(SLOTS - 2, False)
    grads(SLOTS - 1, False)

    for j in range(PIECES):
        for k in range(4):
            first_copy(k, j).wait_send()

    @pl.loop(0, 3 * PIECES)
    def _(i):
        s, j = i // PIECES, lax.rem(i, PIECES)
        for k in range(4):

            @pl.when(s < (3 if k < 2 else 2))
            def _():
                next_copy(k, s, j).wait_send()


def on_device(n, picture_embeddings, description_embeddings, sharpness_factor, offset_term):
    rows, width = picture_embeddings.shape
    vmem = pl.BlockSpec(memory_space=pltpu.VMEM)
    smem = pl.BlockSpec(memory_space=pltpu.SMEM)
    grads = pl.pallas_call(
        functools.partial(kernel, n),
        out_shape=jax.ShapeDtypeStruct((2, width, rows), jnp.float32),
        in_specs=[smem, smem, vmem, vmem],
        out_specs=vmem,
        scratch_shapes=[
            pltpu.VMEM((SLOTS, width, rows), jnp.bfloat16),
            pltpu.VMEM((2, rows, width), jnp.bfloat16),
            pltpu.VMEM((SLOTS, rows, rows), jnp.float32),
            pltpu.VMEM((SLOTS, rows, rows), jnp.float32),
            pltpu.SemaphoreType.DMA((4, PIECES)),
            pltpu.SemaphoreType.DMA((SLOTS, PIECES)),
            pltpu.SemaphoreType.DMA((SLOTS, PIECES)),
            pltpu.SemaphoreType.DMA((SLOTS,)),
            pltpu.SemaphoreType.DMA((SLOTS,)),
        ],
        compiler_params=pltpu.CompilerParams(
            collective_id=0, has_side_effects=True, vmem_limit_bytes=40 * 1024 * 1024
        ),
    )(sharpness_factor, offset_term, picture_embeddings.T, description_embeddings.T)
    return grads[0].T, grads[1].T


def solution(mesh):
    placed = (P("blk", "grp"), P("blk", "grp"), P(), P())
    return jax.shard_map(
        functools.partial(on_device, mesh.shape["blk"]),
        mesh=mesh,
        in_specs=placed,
        out_specs=(P("blk", "grp"), P("blk", "grp")),
        check_vma=False,
    )
```

```python
import functools

import jax
import jax.numpy as jnp
from jax import lax
from jax.experimental import pallas as pl
from jax.experimental.pallas import tpu as pltpu
from jax.sharding import PartitionSpec as P

HOPS = 8
PIECES = 4
WINDOW = 4
DELAY = 4
LAG = 5
EACH = PIECES // 2
SLOTS = 2 * HOPS
STEPS = (HOPS - 1) * PIECES
MESH = pl.DeviceIdType.MESH


def kernel(
    n,
    scale_ref,
    offset_ref,
    image_ref,
    text_ref,
    out_ref,
    blocks,
    own,
    sent,
    got,
    load_sem,
    send_sem,
    recv_sem,
    row_send_sem,
    row_recv_sem,
    core_send_sem,
    core_recv_sem,
):
    me = lax.axis_index("blk")
    core = lax.axis_index("grp")
    width, rows = image_ref.shape
    piece = width // PIECES
    place = lax.rem(me, HOPS)
    start = me - place
    ahead = start + lax.rem(place + 1, HOPS)
    behind = start + lax.rem(place + HOPS - 1, HOPS)
    above, below = lax.rem(me + HOPS, n), lax.rem(me + n - HOPS, n)
    partner = (me, 1 - core)

    loads = [
        pltpu.make_async_copy(text_ref, blocks.at[0, 0], load_sem.at[0]),
        pltpu.make_async_copy(image_ref, blocks.at[0, 1], load_sem.at[1]),
    ]
    for load in loads:
        load.start()
    barrier = pltpu.get_barrier_semaphore()
    others = [(ahead, core), (behind, core), (above, core), (below, core), partner]
    for other in others:
        pl.semaphore_signal(barrier, inc=1, device_id=other, device_id_type=MESH)
    out_ref[...] = jnp.zeros_like(out_ref)
    for load in loads:
        load.wait()
    pl.semaphore_wait(barrier, len(others))

    def part(j):
        return pl.ds(pl.multiple_of(j * piece, 16), piece)

    def ring_copy(q, d):
        r, j = q // PIECES, lax.rem(q, PIECES)
        t = 2 + 2 * r + d
        return pltpu.make_async_remote_copy(
            src_ref=blocks.at[0, jnp.where(r < 2, lax.rem(r + d, 2), t - 4), part(j)],
            dst_ref=blocks.at[0, t, part(j)],
            send_sem=send_sem.at[d, lax.rem(q, WINDOW)],
            recv_sem=recv_sem.at[t, j],
            device_id=(behind if d else ahead, core),
            device_id_type=MESH,
        )

    def row_copy(t, where, to):
        return pltpu.make_async_remote_copy(
            src_ref=blocks.at[0, t, where],
            dst_ref=blocks.at[1, t, where],
            send_sem=row_send_sem.at[t],
            recv_sem=row_recv_sem.at[t],
            device_id=(to, core),
            device_id_type=MESH,
        )

    def elsewhere(t):
        r, d = t // 2 - 1, lax.rem(t, 2)
        s = r // 2
        wrapped = jnp.where(d == 0, place - 1 - s < 0, place + 1 + s >= HOPS)
        return (t >= 2) & (wrapped == (lax.rem(r, 2) == 0))

    def side(t):
        return jnp.where(t < 2, t, lax.rem(t // 2 + 1 + lax.rem(t, 2), 2))

    def core_copy(t):
        return pltpu.make_async_remote_copy(
            src_ref=sent.at[t],
            dst_ref=got.at[t],
            send_sem=core_send_sem.at[t],
            recv_sem=core_recv_sem.at[t],
            device_id=partner,
            device_id_type=MESH,
        )

    def arrive(q):
        r, j = q // PIECES, lax.rem(q, PIECES)
        for d in range(2):
            ring_copy(q, d).wait_recv()
            t = 2 + 2 * r + d

            @pl.when(elsewhere(t))
            def _():
                row_copy(t, part(j), jnp.where(side(t) == 0, above, below)).start()

    def dots(t):
        other = elsewhere(t)

        @pl.when(other)
        def _():
            row_copy(t, pl.ds(0, width), above).wait_recv()

        block = blocks[jnp.where(other, 1, 0), t]
        sent[t] = jnp.dot(own[side(t)], block, preferred_element_type=jnp.float32)
        core_copy(t).start()

    def grads(t):
        core_copy(t).wait()
        probs = jax.nn.sigmoid(scale * (sent[t] + got[t]) + offset)
        row = lax.broadcasted_iota(jnp.int32, (rows, rows), 0)
        column = lax.broadcasted_iota(jnp.int32, (rows, rows), 1)
        match = jnp.where(t < 2, 1.0, 0.0)
        probs = probs - jnp.where(row == column, match, 0.0)
        weight = (scale * probs).astype(jnp.bfloat16)
        block = blocks[jnp.where(elsewhere(t), 1, 0), t]
        out_ref[side(t)] += lax.dot_general(
            block, weight, (((1,), (1,)), ((), ())), preferred_element_type=jnp.float32
        )

    for q in range(WINDOW):
        for d in range(2):
            ring_copy(q, d).start()

    own[0] = blocks[0, 1].T
    own[1] = blocks[0, 0].T
    scale, offset = scale_ref[0], offset_ref[0]

    @pl.loop(WINDOW, STEPS)
    def _(q):
        for d in range(2):
            ring_copy(q - WINDOW, d).wait_send()
            ring_copy(q, d).start()

        @pl.when(q >= DELAY)
        def _():
            arrive(q - DELAY)

        t = (q - LAG) // EACH

        @pl.when((q >= LAG) & (lax.rem(q - LAG, EACH) == 0))
        def _():
            dots(t)

            @pl.when(t > 0)
            def _():
                grads(t - 1)

    @pl.loop(STEPS - DELAY, STEPS)
    def _(q):
        arrive(q)

    @pl.loop((STEPS - 1 - LAG) // EACH + 1, SLOTS + 1)
    def _(t):
        @pl.when(t < SLOTS)
        def _():
            dots(t)

        grads(t - 1)

    for q in range(STEPS - WINDOW, STEPS):
        for d in range(2):
            ring_copy(q, d).wait_send()

    @pl.loop(2, SLOTS)
    def _(t):
        @pl.when(elsewhere(t))
        def _():
            row_copy(t, pl.ds(0, width), above).wait_send()


def on_device(n, picture_embeddings, description_embeddings, sharpness_factor, offset_term):
    rows, width = picture_embeddings.shape
    hbm = pl.BlockSpec(memory_space=pl.ANY)
    vmem = pl.BlockSpec(memory_space=pltpu.VMEM)
    smem = pl.BlockSpec(memory_space=pltpu.SMEM)
    grads = pl.pallas_call(
        functools.partial(kernel, n),
        out_shape=jax.ShapeDtypeStruct((2, width, rows), jnp.float32),
        in_specs=[smem, smem, hbm, hbm],
        out_specs=vmem,
        scratch_shapes=[
            pltpu.VMEM((2, SLOTS, width, rows), jnp.bfloat16),
            pltpu.VMEM((2, rows, width), jnp.bfloat16),
            pltpu.VMEM((SLOTS, rows, rows), jnp.float32),
            pltpu.VMEM((SLOTS, rows, rows), jnp.float32),
            pltpu.SemaphoreType.DMA((2,)),
            pltpu.SemaphoreType.DMA((2, WINDOW)),
            pltpu.SemaphoreType.DMA((SLOTS, PIECES)),
            pltpu.SemaphoreType.DMA((SLOTS,)),
            pltpu.SemaphoreType.DMA((SLOTS,)),
            pltpu.SemaphoreType.DMA((SLOTS,)),
            pltpu.SemaphoreType.DMA((SLOTS,)),
        ],
        compiler_params=pltpu.CompilerParams(
            collective_id=0, has_side_effects=True, vmem_limit_bytes=40 * 1024 * 1024
        ),
    )(sharpness_factor, offset_term, picture_embeddings.T, description_embeddings.T)
    return grads[0].T, grads[1].T


def solution(mesh):
    placed = (P("blk", "grp"), P("blk", "grp"), P(), P())
    return jax.shard_map(
        functools.partial(on_device, mesh.shape["blk"]),
        mesh=mesh,
        in_specs=placed,
        out_specs=(P("blk", "grp"), P("blk", "grp")),
        check_vma=False,
    )
```

```python
import functools

import jax
import jax.numpy as jnp
from jax import lax
from jax.experimental import pallas as pl
from jax.experimental.pallas import tpu as pltpu
from jax.sharding import PartitionSpec as P

HOPS = 8
PIECES = 4
WINDOW = 4
DELAY = 4
LAG = 19
HELD = 7
LAYERS = 12
SLOTS = 2 * HOPS
STEPS = (HOPS - 1) * PIECES
MESH = pl.DeviceIdType.MESH


def kernel(
    n,
    scale_ref,
    offset_ref,
    image_ref,
    text_ref,
    out_ref,
    blocks,
    own,
    sent,
    got,
    load_sem,
    send_sem,
    recv_sem,
    row_send_sem,
    row_recv_sem,
    ready_sem,
    core_send_sem,
    core_recv_sem,
):
    me = lax.axis_index("blk")
    core = lax.axis_index("grp")
    width, rows = image_ref.shape
    piece = width // PIECES
    place = lax.rem(me, HOPS)
    start = me - place
    ahead = start + lax.rem(place + 1, HOPS)
    behind = start + lax.rem(place + HOPS - 1, HOPS)
    above, below = lax.rem(me + HOPS, n), lax.rem(me + n - HOPS, n)
    partner = (me, 1 - core)
    first = lax.rem(me // HOPS, LAYERS) == 0
    held = jnp.where(first, HELD, 0)

    loads = [
        pltpu.make_async_copy(text_ref, blocks.at[0, 0], load_sem.at[0]),
        pltpu.make_async_copy(image_ref, blocks.at[0, 1], load_sem.at[1]),
    ]
    for load in loads:
        load.start()
    barrier = pltpu.get_barrier_semaphore()
    others = [(ahead, core), (behind, core), (below, core), partner]
    for other in others:
        pl.semaphore_signal(barrier, inc=1, device_id=other, device_id_type=MESH)
    out_ref[...] = jnp.zeros_like(out_ref)
    for load in loads:
        load.wait()
    pl.semaphore_wait(barrier, len(others))
    pl.semaphore_signal(ready_sem, inc=1, device_id=(above, core), device_id_type=MESH)

    def part(j):
        return pl.ds(pl.multiple_of(j * piece, 16), piece)

    def ring_copy(q, d):
        r, j = q // PIECES, lax.rem(q, PIECES)
        t = 2 + 2 * r + d
        return pltpu.make_async_remote_copy(
            src_ref=blocks.at[0, jnp.where(r < 2, lax.rem(r + d, 2), t - 4), part(j)],
            dst_ref=blocks.at[0, t, part(j)],
            send_sem=send_sem.at[d, lax.rem(q, WINDOW)],
            recv_sem=recv_sem.at[t, j],
            device_id=(behind if d else ahead, core),
            device_id_type=MESH,
        )

    def row_copy(t, where, to):
        return pltpu.make_async_remote_copy(
            src_ref=blocks.at[0, t, where],
            dst_ref=blocks.at[1, t, where],
            send_sem=row_send_sem.at[t],
            recv_sem=row_recv_sem.at[t],
            device_id=(to, core),
            device_id_type=MESH,
        )

    def elsewhere(t):
        r, d = t // 2 - 1, lax.rem(t, 2)
        s = r // 2
        wrapped = jnp.where(d == 0, place - 1 - s < 0, place + 1 + s >= HOPS)
        return (t >= 2) & (wrapped == (lax.rem(r, 2) == 0))

    def side(t):
        return jnp.where(t < 2, t, lax.rem(t // 2 + 1 + lax.rem(t, 2), 2))

    def core_copy(t):
        return pltpu.make_async_remote_copy(
            src_ref=sent.at[t],
            dst_ref=got.at[t],
            send_sem=core_send_sem.at[t],
            recv_sem=core_recv_sem.at[t],
            device_id=partner,
            device_id_type=MESH,
        )

    def pass_down(q, d):
        r, j = q // PIECES, lax.rem(q, PIECES)
        t = 2 + 2 * r + d

        @pl.when(elsewhere(t) & (side(t) == 1))
        def _():
            row_copy(t, part(j), below).start()

    def arrive(q):
        r, j = q // PIECES, lax.rem(q, PIECES)

        @pl.when(q == held)
        def _():
            pl.semaphore_wait(ready_sem, 1)

            @pl.when(first)
            def _():
                @pl.loop(0, HELD)
                def _(past):
                    for d in range(2):
                        pass_down(past, d)

        for d in range(2):
            ring_copy(q, d).wait_recv()
            t = 2 + 2 * r + d

            @pl.when(elsewhere(t) & (side(t) == 0))
            def _():
                row_copy(t, part(j), above).start()

            @pl.when(q >= held)
            def _():
                pass_down(q, d)

    def put_off(t):
        return first & elsewhere(t) & (side(t) == 0)

    def dots(t):
        other = elsewhere(t)

        @pl.when(other)
        def _():
            row_copy(t, pl.ds(0, width), above).wait_recv()

        block = blocks[jnp.where(other, 1, 0), t]
        sent[t] = jnp.dot(own[side(t)], block, preferred_element_type=jnp.float32)
        core_copy(t).start()

    def grads(t):
        core_copy(t).wait()
        probs = jax.nn.sigmoid(scale * (sent[t] + got[t]) + offset)
        row = lax.broadcasted_iota(jnp.int32, (rows, rows), 0)
        column = lax.broadcasted_iota(jnp.int32, (rows, rows), 1)
        match = jnp.where(t < 2, 1.0, 0.0)
        probs = probs - jnp.where(row == column, match, 0.0)
        weight = (scale * probs).astype(jnp.bfloat16)
        block = blocks[jnp.where(elsewhere(t), 1, 0), t]
        out_ref[side(t)] += lax.dot_general(
            block, weight, (((1,), (1,)), ((), ())), preferred_element_type=jnp.float32
        )

    def products(t, apart, chosen):
        @pl.when((t < SLOTS) & chosen(t))
        def _():
            dots(t)

        @pl.when((t >= apart) & chosen(t - apart))
        def _():
            grads(t - apart)

    for q in range(WINDOW):
        for d in range(2):
            ring_copy(q, d).start()

    own[0] = blocks[0, 1].T
    own[1] = blocks[0, 0].T
    scale, offset = scale_ref[0], offset_ref[0]

    @pl.loop(WINDOW, STEPS + DELAY)
    def _(q):
        @pl.when(q < STEPS)
        def _():
            for d in range(2):
                ring_copy(q - WINDOW, d).wait_send()
                ring_copy(q, d).start()

        @pl.when(q >= DELAY)
        def _():
            arrive(q - DELAY)

        @pl.when(q >= LAG)
        def _():
            products(q - LAG, 1, lambda t: ~put_off(t))

    @pl.loop(STEPS + DELAY - LAG, SLOTS + 1)
    def _(t):
        products(t, 1, lambda t: ~put_off(t))

    @pl.when(first)
    def _():
        @pl.loop(2, SLOTS + 4)
        def _(t):
            products(t, 4, put_off)

    for q in range(STEPS - WINDOW, STEPS):
        for d in range(2):
            ring_copy(q, d).wait_send()

    @pl.loop(2, SLOTS)
    def _(t):
        @pl.when(elsewhere(t))
        def _():
            row_copy(t, pl.ds(0, width), above).wait_send()


def on_device(n, picture_embeddings, description_embeddings, sharpness_factor, offset_term):
    rows, width = picture_embeddings.shape
    hbm = pl.BlockSpec(memory_space=pl.ANY)
    vmem = pl.BlockSpec(memory_space=pltpu.VMEM)
    smem = pl.BlockSpec(memory_space=pltpu.SMEM)
    grads = pl.pallas_call(
        functools.partial(kernel, n),
        out_shape=jax.ShapeDtypeStruct((2, width, rows), jnp.float32),
        in_specs=[smem, smem, hbm, hbm],
        out_specs=vmem,
        scratch_shapes=[
            pltpu.VMEM((2, SLOTS, width, rows), jnp.bfloat16),
            pltpu.VMEM((2, rows, width), jnp.bfloat16),
            pltpu.VMEM((SLOTS, rows, rows), jnp.float32),
            pltpu.VMEM((SLOTS, rows, rows), jnp.float32),
            pltpu.SemaphoreType.DMA((2,)),
            pltpu.SemaphoreType.DMA((2, WINDOW)),
            pltpu.SemaphoreType.DMA((SLOTS, PIECES)),
            pltpu.SemaphoreType.DMA((SLOTS,)),
            pltpu.SemaphoreType.DMA((SLOTS,)),
            pltpu.SemaphoreType.REGULAR,
            pltpu.SemaphoreType.DMA((SLOTS,)),
            pltpu.SemaphoreType.DMA((SLOTS,)),
        ],
        compiler_params=pltpu.CompilerParams(
            collective_id=0, has_side_effects=True, vmem_limit_bytes=40 * 1024 * 1024
        ),
    )(sharpness_factor, offset_term, picture_embeddings.T, description_embeddings.T)
    return grads[0].T, grads[1].T


def solution(mesh):
    placed = (P("blk", "grp"), P("blk", "grp"), P(), P())
    return jax.shard_map(
        functools.partial(on_device, mesh.shape["blk"]),
        mesh=mesh,
        in_specs=placed,
        out_specs=(P("blk", "grp"), P("blk", "grp")),
        check_vma=False,
    )
```

```python
import functools

import jax
import jax.numpy as jnp
from jax import lax
from jax.experimental import pallas as pl
from jax.experimental.pallas import tpu as pltpu
from jax.sharding import PartitionSpec as P

HOPS = 8
PIECES = 4
WINDOW = 3
DELAY = 3
LAG = 19
HELD = 7
LAYERS = 12
SLOTS = 2 * HOPS
STEPS = (HOPS - 1) * PIECES
MESH = pl.DeviceIdType.MESH


def kernel(
    n,
    scale_ref,
    offset_ref,
    image_ref,
    text_ref,
    out_ref,
    blocks,
    own,
    sent,
    got,
    load_sem,
    send_sem,
    recv_sem,
    row_send_sem,
    row_recv_sem,
    ready_sem,
    core_send_sem,
    core_recv_sem,
):
    me = lax.axis_index("blk")
    core = lax.axis_index("grp")
    width, rows = image_ref.shape
    piece = width // PIECES
    place = lax.rem(me, HOPS)
    start = me - place
    ahead = start + lax.rem(place + 1, HOPS)
    behind = start + lax.rem(place + HOPS - 1, HOPS)
    above, below = lax.rem(me + HOPS, n), lax.rem(me + n - HOPS, n)
    partner = (me, 1 - core)
    first = lax.rem(me // HOPS, LAYERS) == 0
    held = jnp.where(first, HELD, 0)

    loads = [
        pltpu.make_async_copy(text_ref, blocks.at[0, 0], load_sem.at[0]),
        pltpu.make_async_copy(image_ref, blocks.at[0, 1], load_sem.at[1]),
    ]
    for load in loads:
        load.start()
    barrier = pltpu.get_barrier_semaphore()
    others = [(ahead, core), (behind, core), (below, core), partner]
    for other in others:
        pl.semaphore_signal(barrier, inc=1, device_id=other, device_id_type=MESH)
    out_ref[...] = jnp.zeros_like(out_ref)
    for load in loads:
        load.wait()
    pl.semaphore_wait(barrier, len(others))
    pl.semaphore_signal(ready_sem, inc=1, device_id=(above, core), device_id_type=MESH)

    def part(j):
        return pl.ds(pl.multiple_of(j * piece, 16), piece)

    def source(r, d):
        t = 2 + 2 * r + d
        if d:
            return jnp.where(r < 2, 1 - r, t - 4)
        return jnp.where(r == 0, 0, jnp.where(r == 1, 2, jnp.where(r == 2, 1, t - 4)))

    def ring_copy(q, d):
        r, j = q // PIECES, lax.rem(q, PIECES)
        t = 2 + 2 * r + d
        return pltpu.make_async_remote_copy(
            src_ref=blocks.at[0, source(r, d), part(j)],
            dst_ref=blocks.at[0, t, part(j)],
            send_sem=send_sem.at[d, lax.rem(q, WINDOW)],
            recv_sem=recv_sem.at[t, j],
            device_id=(behind if d else ahead, core),
            device_id_type=MESH,
        )

    def row_copy(t, where, to):
        return pltpu.make_async_remote_copy(
            src_ref=blocks.at[0, t, where],
            dst_ref=blocks.at[1, t, where],
            send_sem=row_send_sem.at[t],
            recv_sem=row_recv_sem.at[t],
            device_id=(to, core),
            device_id_type=MESH,
        )

    def elsewhere(t):
        r, d = t // 2 - 1, lax.rem(t, 2)
        caption = side(t) == 0
        s = jnp.where(d == 1, r // 2, jnp.where(caption, (r + 1) // 2, r // 2 - 1))
        wrapped = jnp.where(d == 0, place - 1 - s < 0, place + 1 + s >= HOPS)
        return (t >= 2) & (wrapped == ((d == 0) == caption))

    def side(t):
        r, d = t // 2 - 1, lax.rem(t, 2)
        image = jnp.where((d == 0) & (r == 0), 0, 1 - lax.rem(r, 2))
        return jnp.where(t < 2, t, image)

    def core_copy(t):
        return pltpu.make_async_remote_copy(
            src_ref=sent.at[t],
            dst_ref=got.at[t],
            send_sem=core_send_sem.at[t],
            recv_sem=core_recv_sem.at[t],
            device_id=partner,
            device_id_type=MESH,
        )

    def pass_down(q, d):
        r, j = q // PIECES, lax.rem(q, PIECES)
        t = 2 + 2 * r + d

        @pl.when(elsewhere(t) & (side(t) == 1))
        def _():
            row_copy(t, part(j), below).start()

    def arrive(q):
        r, j = q // PIECES, lax.rem(q, PIECES)

        @pl.when(q == held)
        def _():
            pl.semaphore_wait(ready_sem, 1)

            @pl.when(first)
            def _():
                @pl.loop(0, HELD)
                def _(past):
                    for d in range(2):
                        pass_down(past, d)

        for d in range(2):
            ring_copy(q, d).wait_recv()
            t = 2 + 2 * r + d

            @pl.when(elsewhere(t) & (side(t) == 0))
            def _():
                row_copy(t, part(j), above).start()

            @pl.when(q >= held)
            def _():
                pass_down(q, d)

    def put_off(t):
        return first & elsewhere(t) & (side(t) == 0)

    def dots(t):
        other = elsewhere(t)

        @pl.when(other)
        def _():
            row_copy(t, pl.ds(0, width), above).wait_recv()

        block = blocks[jnp.where(other, 1, 0), t]
        sent[t] = jnp.dot(own[side(t)], block, preferred_element_type=jnp.float32)
        core_copy(t).start()

    def grads(t):
        core_copy(t).wait()
        probs = jax.nn.sigmoid(scale * (sent[t] + got[t]) + offset)
        row = lax.broadcasted_iota(jnp.int32, (rows, rows), 0)
        column = lax.broadcasted_iota(jnp.int32, (rows, rows), 1)
        match = jnp.where(t < 2, 1.0, 0.0)
        probs = probs - jnp.where(row == column, match, 0.0)
        weight = (scale * probs).astype(jnp.bfloat16)
        block = blocks[jnp.where(elsewhere(t), 1, 0), t]
        out_ref[side(t)] += lax.dot_general(
            block, weight, (((1,), (1,)), ((), ())), preferred_element_type=jnp.float32
        )

    def products(t, apart, chosen):
        @pl.when((t < SLOTS) & chosen(t))
        def _():
            dots(t)

        @pl.when((t >= apart) & chosen(t - apart))
        def _():
            grads(t - apart)

    for q in range(WINDOW):
        for d in range(2):
            ring_copy(q, d).start()

    own[0] = blocks[0, 1].T
    own[1] = blocks[0, 0].T
    scale, offset = scale_ref[0], offset_ref[0]

    @pl.loop(WINDOW, STEPS + DELAY)
    def _(q):
        @pl.when(q < STEPS)
        def _():
            for d in range(2):
                ring_copy(q - WINDOW, d).wait_send()
                ring_copy(q, d).start()

        @pl.when(q >= DELAY)
        def _():
            arrive(q - DELAY)

        @pl.when(q >= LAG)
        def _():
            products(q - LAG, 1, lambda t: ~put_off(t))

    @pl.loop(STEPS + DELAY - LAG, SLOTS + 1)
    def _(t):
        products(t, 1, lambda t: ~put_off(t))

    @pl.when(first)
    def _():
        @pl.loop(2, SLOTS + 4)
        def _(t):
            products(t, 4, put_off)

    for q in range(STEPS - WINDOW, STEPS):
        for d in range(2):
            ring_copy(q, d).wait_send()

    @pl.loop(2, SLOTS)
    def _(t):
        @pl.when(elsewhere(t))
        def _():
            row_copy(t, pl.ds(0, width), above).wait_send()


def on_device(n, picture_embeddings, description_embeddings, sharpness_factor, offset_term):
    rows, width = picture_embeddings.shape
    hbm = pl.BlockSpec(memory_space=pl.ANY)
    vmem = pl.BlockSpec(memory_space=pltpu.VMEM)
    smem = pl.BlockSpec(memory_space=pltpu.SMEM)
    grads = pl.pallas_call(
        functools.partial(kernel, n),
        out_shape=jax.ShapeDtypeStruct((2, width, rows), jnp.float32),
        in_specs=[smem, smem, hbm, hbm],
        out_specs=vmem,
        scratch_shapes=[
            pltpu.VMEM((2, SLOTS, width, rows), jnp.bfloat16),
            pltpu.VMEM((2, rows, width), jnp.bfloat16),
            pltpu.VMEM((SLOTS, rows, rows), jnp.float32),
            pltpu.VMEM((SLOTS, rows, rows), jnp.float32),
            pltpu.SemaphoreType.DMA((2,)),
            pltpu.SemaphoreType.DMA((2, WINDOW)),
            pltpu.SemaphoreType.DMA((SLOTS, PIECES)),
            pltpu.SemaphoreType.DMA((SLOTS,)),
            pltpu.SemaphoreType.DMA((SLOTS,)),
            pltpu.SemaphoreType.REGULAR,
            pltpu.SemaphoreType.DMA((SLOTS,)),
            pltpu.SemaphoreType.DMA((SLOTS,)),
        ],
        compiler_params=pltpu.CompilerParams(
            collective_id=0, has_side_effects=True, vmem_limit_bytes=40 * 1024 * 1024
        ),
    )(sharpness_factor, offset_term, picture_embeddings.T, description_embeddings.T)
    return grads[0].T, grads[1].T


def solution(mesh):
    placed = (P("blk", "grp"), P("blk", "grp"), P(), P())
    return jax.shard_map(
        functools.partial(on_device, mesh.shape["blk"]),
        mesh=mesh,
        in_specs=placed,
        out_specs=(P("blk", "grp"), P("blk", "grp")),
        check_vma=False,
    )
```
